32 devices in a mesh: row: 4 (over y, x), col: 4 (over z), rep: 2 (over core).
Axes of the slice: x: 2, y: 2, z: 4, core: 2. Of those that a mesh axis runs over, the one named last changes fastest.
Arguments:
- features: bfloat16 [2, 2048, 512], P('rep', ('row', 'col')), may hold values from -6 to 6
- cotangent: bfloat16 [2, 2048, 512], P('rep', ('row', 'col')), may hold values from -6 to 6
- weight: bfloat16 [512, 512], replicated, may hold values from -0.25 to 0.25
- tile_values: bfloat16 [2, 256, 128, 128], P('rep', ('row', 'col')), may hold values from -0.25 to 0.25
- tile_out: int32 [2, 256], P('rep', ('row', 'col')), may hold values from 0 to 3
- tile_in: int32 [2, 256], P('rep', ('row', 'col')), may hold values from 0 to 3
- tile_count: int32 [2, 16], P('rep', ('row', 'col')), may hold values from 8 to 16, as said below
Outputs:
- out_feats: bfloat16 [2, 2048, 512], P('rep', ('row', 'col'))
- grad_feats: bfloat16 [2, 2048, 512], P('rep', ('row', 'col'))
- grad_weight: float32 [512, 512], replicated
The draws below stay inside these ranges and needn't reach their ends.
Inputs may be any that keep to these rules, and one draw needn't show every extreme that they name: `tile_count`: in each window some group has all 16 slots live.
All inputs are finite; a program needn't handle non-finite values.
Results may differ from the reference program's by a relative error of at most 0.015.
Values may be sent and summed in bfloat16 or wider, within the bound.
A program may use at most 64 MiB of HBM per device.

```python
import jax
import jax.numpy as jnp
from jax import lax

F = 512
BLOCK = 128
NODE_DEV = 128
SECTIONS = 4
TILE_CAP = 16
ROW_DEVS = 4
COL_DEVS = 4
WINDOWS = 2
SLOTS = 16
NODES = 2048
TILES = 256
OUT_BLOCKS = 4
IN_BLOCKS = 4


def draw_tile_count(key, part):
    first_key, second_key = jax.random.split(jax.random.fold_in(key, 11))
    base = jax.random.randint(first_key, (WINDOWS, SLOTS), TILE_CAP // 2, TILE_CAP + 1)
    chosen = jax.random.randint(second_key, (WINDOWS, 1), 0, SLOTS)
    filled = jnp.arange(SLOTS, dtype=jnp.int32)[None, :] == chosen
    return jnp.where(filled, TILE_CAP, base).astype(jnp.int32)


def touch_ends(result, own_key, smallest, largest):
    place = [jax.random.randint(jax.random.fold_in(own_key, axis), (), 0, length) for axis, length in enumerate(result.shape)]
    longest = result.shape.index(max(result.shape))
    next_to = place[:longest] + [(place[longest] + 1) % result.shape[longest]] + place[longest + 1:]
    return result.at[tuple(place)].set(smallest).at[tuple(next_to)].set(largest)


def levels(stream_key, shape, cuts, smallest, largest):
    def one(axis_at, blocks):
        heights = jax.random.uniform(jax.random.fold_in(jax.random.fold_in(stream_key, 6), axis_at), (blocks,), jnp.float32, smallest / len(cuts), largest / len(cuts))
        return jnp.repeat(jnp.exp(heights), shape[axis_at] // blocks).reshape((-1,) + (1,) * (len(shape) - axis_at - 1))

    level = one(*cuts[0])
    for cut in cuts[1:]:
        level = level * one(*cut)
    return level


def noise(rng, extent, deviation, reach, shards=(), kind=jnp.bfloat16):
    drawn = deviation * jax.random.normal(rng, extent, jnp.float32)
    if shards:
        drawn = drawn * levels(rng, extent, shards, -0.22, 0.18)
    return jnp.clip(drawn, -reach, reach).astype(kind)


def setup_inputs(seed: int = 0) -> dict:
    arg_keys = jax.random.split(jax.random.key(seed), 8)
    features = noise(arg_keys[0], (WINDOWS, NODES, F), 1.0, 6.0, ((0, 2), (1, 16)))
    cotangent = noise(arg_keys[1], (WINDOWS, NODES, F), 1.0, 6.0, ((0, 2), (1, 16)))
    weight = noise(arg_keys[2], (F, F), F ** -0.5, 0.25)
    tile_values = noise(arg_keys[3], (WINDOWS, TILES, BLOCK, BLOCK), (TILE_CAP * BLOCK // OUT_BLOCKS) ** -0.5, 0.25, ((0, 2), (1, 16)))
    tile_out = touch_ends(jax.random.randint(arg_keys[4], (WINDOWS, TILES), 0, OUT_BLOCKS), jax.random.fold_in(arg_keys[4], 1), 0, OUT_BLOCKS - 1).astype(jnp.int32)
    tile_in = touch_ends(jax.random.randint(arg_keys[5], (WINDOWS, TILES), 0, IN_BLOCKS), jax.random.fold_in(arg_keys[5], 1), 0, IN_BLOCKS - 1).astype(jnp.int32)
    tile_count = draw_tile_count(jax.random.fold_in(arg_keys[7], 71), 0)
    return dict(features=features, cotangent=cotangent, weight=weight, tile_values=tile_values, tile_out=tile_out, tile_in=tile_in, tile_count=tile_count)


def grids(values, outs_idx, ins_idx, counts):
    values_grid = values.reshape(ROW_DEVS * COL_DEVS, TILE_CAP, BLOCK, BLOCK)
    outs_grid = outs_idx.reshape(ROW_DEVS * COL_DEVS, TILE_CAP)
    ins_grid = ins_idx.reshape(ROW_DEVS * COL_DEVS, TILE_CAP)
    return values_grid, outs_grid, ins_grid, counts


def propagate(field, values, outs_idx, ins_idx, counts):
    half = SECTIONS // 2
    spans = field.reshape(ROW_DEVS, COL_DEVS, NODE_DEV, F)
    padded = jnp.pad(spans, ((half, SECTIONS - 1 - half), (0, 0), (0, 0), (0, 0)))
    values_grid, outs_grid, ins_grid, count_grid = grids(values, outs_idx, ins_idx, counts)
    slot_ids = jnp.arange(TILE_CAP, dtype=jnp.int32)
    block_ids = jnp.arange(OUT_BLOCKS, dtype=jnp.int32)

    def one_row(row_id):
        def one_group(col_id):
            group = row_id * COL_DEVS + col_id
            segment_in = lax.dynamic_slice(padded, (row_id, col_id, jnp.int32(0), jnp.int32(0)), (SECTIONS, 1, NODE_DEV, F))
            blocks = segment_in.reshape(IN_BLOCKS, BLOCK, F)
            picked = blocks[ins_grid[group]]
            prods = jnp.einsum('tij,tjf->tif', values_grid[group].astype(jnp.float32), picked.astype(jnp.float32))
            live = (slot_ids < count_grid[group]).astype(jnp.float32)
            hot = (outs_grid[group][None, :] == block_ids[:, None]).astype(jnp.float32) * live[None, :]
            part = jnp.einsum('ot,tif->oif', hot, prods, precision=lax.Precision.HIGHEST)
            part = part.reshape(OUT_BLOCKS * BLOCK, F)
            return lax.optimization_barrier(part.astype(jnp.bfloat16)).astype(jnp.float32)

        parts = lax.map(one_group, jnp.arange(COL_DEVS, dtype=jnp.int32))
        return jnp.sum(parts, axis=0).astype(jnp.bfloat16)

    rows = lax.map(one_row, jnp.arange(ROW_DEVS, dtype=jnp.int32))
    return rows.reshape(NODES, F)


def adjoint(field, values, outs_idx, ins_idx, counts):
    half = SECTIONS // 2
    row_fields = field.reshape(ROW_DEVS, OUT_BLOCKS, BLOCK, F)
    values_grid, outs_grid, ins_grid, count_grid = grids(values, outs_idx, ins_idx, counts)
    slot_ids = jnp.arange(TILE_CAP, dtype=jnp.int32)
    block_ids = jnp.arange(IN_BLOCKS, dtype=jnp.int32)

    def one_group(total, group):
        row_id = group // COL_DEVS
        col_id = group % COL_DEVS
        blocks = row_fields[row_id]
        picked = blocks[outs_grid[group]]
        prods = jnp.einsum('tij,tif->tjf', values_grid[group].astype(jnp.float32), picked.astype(jnp.float32))
        live = (slot_ids < count_grid[group]).astype(jnp.float32)
        hot = (ins_grid[group][None, :] == block_ids[:, None]).astype(jnp.float32) * live[None, :]
        part = jnp.einsum('it,tjf->ijf', hot, prods, precision=lax.Precision.HIGHEST)
        part = part.astype(jnp.bfloat16).astype(jnp.float32).reshape(SECTIONS, 1, NODE_DEV, F)
        start = (row_id.astype(jnp.int32), col_id.astype(jnp.int32), jnp.int32(0), jnp.int32(0))
        current = lax.dynamic_slice(total, start, (SECTIONS, 1, NODE_DEV, F))
        return lax.dynamic_update_slice(total, current + part, start), None

    padded = jnp.zeros((ROW_DEVS + SECTIONS - 1, COL_DEVS, NODE_DEV, F), jnp.float32)
    padded, unused = lax.scan(one_group, padded, jnp.arange(ROW_DEVS * COL_DEVS, dtype=jnp.int32))
    return padded[half:half + ROW_DEVS].reshape(NODES, F).astype(jnp.bfloat16)


def reference(features, cotangent, weight, tile_values, tile_out, tile_in, tile_count):
    outs_list = []
    grads_list = []
    grad_total = jnp.zeros((F, F), jnp.float32)
    for window in range(WINDOWS):
        args = (tile_values[window], tile_out[window], tile_in[window], tile_count[window])
        hidden = propagate(features[window], *args)
        pre = jnp.dot(hidden, weight, preferred_element_type=jnp.float32)
        outs_list.append(jax.nn.silu(pre).astype(jnp.bfloat16))
        sigma = jax.nn.sigmoid(pre)
        dpre = (cotangent[window].astype(jnp.float32) * sigma * (1.0 + pre * (1.0 - sigma))).astype(jnp.bfloat16)
        grad_total = grad_total + jnp.dot(hidden.T, dpre, preferred_element_type=jnp.float32)
        dhidden = jnp.dot(dpre, weight.T, preferred_element_type=jnp.float32).astype(jnp.bfloat16)
        grads_list.append(adjoint(dhidden, *args))
    scale = jnp.float32(WINDOWS * NODES) ** -0.5
    return jnp.stack(outs_list), jnp.stack(grads_list), grad_total * scale
```

```python
import functools

import jax
import jax.numpy as jnp
from jax import lax
from jax.experimental import pallas as pl
from jax.experimental.pallas import tpu as pltpu
from jax.sharding import PartitionSpec as P

SECTIONS = 4
HALF = SECTIONS // 2
OTHERS = tuple(s for s in range(SECTIONS) if s != HALF)
CHUNKS = 4
MESH = pl.DeviceIdType.MESH
F32, BF16 = jnp.float32, jnp.bfloat16


def remote(src, dst, send, recv, axis, index):
    return pltpu.make_async_remote_copy(
        src_ref=src, dst_ref=dst, send_sem=send, recv_sem=recv, device_id={axis: index}, device_id_type=MESH
    )


def dot(a, b, dims=((1,), (0,))):
    return lax.dot_general(a, b, (dims, ((), ())), preferred_element_type=F32)


def kernel(
    rows, cols, reps, fused,
    feat, cot, w, vals, touts, tins, tcount,
    out, gfeat, gweight,
    a, at, x, part, arrived, hid, grads, secs, landed,
    mine, rep_in, row_out, row_in, col_out, col_in, full,
    xs, xr, ps, pr, gs, gr, ss, sr, rs, rr, ws, wr, cs, cr, rs2, rr2, ws2, wr2, cs2, cr2,
):
    r, c, p = lax.axis_index("row"), lax.axis_index("col"), lax.axis_index("rep")
    span, width = feat.shape[1:]
    wide = width // CHUNKS
    edge = vals.shape[-1]
    slots = vals.shape[1]
    own = pl.ds(pl.multiple_of(c * span, span), span)

    def sec(s):
        return pl.ds(s * span, span)

    def cut(j):
        return pl.ds(j * wide, wide)

    def inside(index):
        return jnp.logical_and(index >= 0, index < rows)

    def ring(axis, me, count):
        return [(k - 1, axis, lax.rem(me + k, count)) for k in range(1, count)]

    col_peers = ring("col", c, cols)
    row_peers = ring("row", r, rows) if fused else []
    rep_peers = ring("rep", p, reps) if fused else []

    barrier = pltpu.get_barrier_semaphore()
    for _, axis, index in col_peers + row_peers + rep_peers:
        pl.semaphore_signal(barrier, inc=1, device_id={axis: index}, device_id_type=MESH)
    if not fused:
        for d in (-2, -1, 1, 2):
            @pl.when(inside(r + d))
            def _():
                pl.semaphore_signal(barrier, inc=1, device_id={"row": r + d}, device_id_type=MESH)
        for d in (-2, -1, 1, 2):
            @pl.when(inside(r + d))
            def _():
                pl.semaphore_wait(barrier, 1)
    pl.semaphore_wait(barrier, len(col_peers + row_peers + rep_peers))

    def x_copy(j, n, s):
        return remote(feat.at[0, :, cut(j)], x.at[j, sec(s), :], xs.at[j, n], xr.at[j, n], "row", r - (s - HALF))

    for j in range(CHUNKS):
        for n, s in enumerate(OTHERS):
            @pl.when(inside(r - (s - HALF)))
            def _():
                x_copy(j, n, s).start()

    for j in range(CHUNKS):
        x[j, sec(HALF), :] = feat[0, :, j * wide : (j + 1) * wide]
        for n, s in enumerate(OTHERS):
            @pl.when(jnp.logical_not(inside(r + (s - HALF))))
            def _():
                x[j, sec(s), :] = jnp.zeros((span, wide), BF16)

            @pl.when(jnp.logical_not(inside(r - (s - HALF))))
            def _():
                landed[j, n] = jnp.zeros((span, wide), BF16)

    count = tcount[0, 0]
    one, zero = jnp.float32(1), jnp.float32(0)
    hot_out = [[jnp.where(touts[0, t] == o, one, zero) for o in range(cols)] for t in range(slots)]
    hot_in = [
        [jnp.where(jnp.logical_and(tins[0, t] == i, t < count), one, zero) for i in range(SECTIONS)]
        for t in range(slots)
    ]
    strip = 16

    @pl.loop(0, edge // strip)
    def _(step):
        at_row = pl.multiple_of(step * strip, strip)
        total = [[jnp.zeros((strip, edge), F32) for _ in range(SECTIONS)] for _ in range(cols)]
        for t in range(slots):
            v = vals[0, t, pl.ds(at_row, strip), :].astype(F32)
            for i in range(SECTIONS):
                picked = v * hot_in[t][i]
                for o in range(cols):
                    total[o][i] = total[o][i] + picked * hot_out[t][o]
        for o in range(cols):
            for i in range(SECTIONS):
                a[pl.ds(o * edge + at_row, strip), i * edge : (i + 1) * edge] = total[o][i].astype(BF16)

    def part_copy(j, k, axis, index):
        rows_of = pl.ds(pl.multiple_of(index * span, span), span)
        return remote(part.at[j, rows_of, :], arrived.at[j, k], ps.at[j, k], pr.at[j, k], axis, index)

    for j in range(CHUNKS):
        for n, s in enumerate(OTHERS):
            @pl.when(inside(r + (s - HALF)))
            def _():
                x_copy(j, n, s).wait_recv()
        part[j] = dot(a[...], x[j]).astype(BF16)
        for peer in col_peers:
            part_copy(j, *peer).start()

    at[...] = a[...].astype(F32).T.astype(BF16)

    pre = jnp.zeros((span, width), F32)
    for j in range(CHUNKS):
        for peer in col_peers:
            part_copy(j, *peer).wait_recv()
        summed = part[j, own, :].astype(F32)
        for k in range(cols - 1):
            summed = summed + arrived[j, k].astype(F32)
        summed = summed.astype(BF16)
        hid[:, j * wide : (j + 1) * wide] = summed
        pre = pre + dot(summed, w[j * wide : (j + 1) * wide, :])

    sigma = jax.nn.sigmoid(pre)
    dpre = (cot[0].astype(F32) * sigma * (1.0 + pre * (1.0 - sigma))).astype(BF16)

    def grad_copy(j, k, axis, index):
        return remote(grads.at[j, own, :], grads.at[j, own, :], gs.at[j, k], gr.at[j, k], axis, index)

    def grad_wait(j, k):
        source = pl.ds(pl.multiple_of(lax.rem(c + cols - 1 - k, cols) * span, span), span)
        remote(grads.at[j, source, :], grads.at[j, source, :], gs.at[j, k], gr.at[j, k], "col", col_peers[k][2]).wait_recv()

    for j in range(CHUNKS):
        grads[j, own, :] = dot(dpre, w[j * wide : (j + 1) * wide, :], ((1,), (1,))).astype(BF16)
        for peer in col_peers:
            grad_copy(j, *peer).start()
    out[0] = (pre * sigma).astype(BF16)

    scale = float(span * rows * cols * reps) ** -0.5
    term = dot(hid[...].astype(F32).T.astype(BF16), dpre) * scale
    if not fused:
        gweight[...] = term
    else:
        mine[...] = term.astype(BF16)
        rep_rows = width // reps
        row_rows = rep_rows // rows
        col_rows = row_rows // cols

        def piece(size, index):
            return pl.ds(pl.multiple_of(index * size, size), size)

        def rep_copy(k, axis, index):
            return remote(mine.at[piece(rep_rows, index), :], rep_in.at[k], rs.at[k], rr.at[k], axis, index)

        def row_copy(k, axis, index):
            return remote(row_out.at[piece(row_rows, index), :], row_in.at[k], ws.at[k], wr.at[k], axis, index)

        def col_copy(k, axis, index):
            return remote(col_out.at[piece(col_rows, index), :], col_in.at[k], cs.at[k], cr.at[k], axis, index)

        def place(level, p, r, c):
            start = p * rep_rows
            if level < 2:
                start = start + r * row_rows
            if level < 1:
                start = start + c * col_rows
            size = (col_rows, row_rows, rep_rows)[level]
            return full.at[pl.ds(pl.multiple_of(start, size), size), :]

        def back_copy(level, k, axis, index, arriving=False):
            send, recv = ((cs2, cr2), (ws2, wr2), (rs2, rr2))[level]
            where = [p, r, c]
            if arriving:
                which = ("rep", "row", "col").index(axis)
                total = (reps, rows, cols)[which]
                where[which] = lax.rem(where[which] + total - 1 - k, total)
            spot = place(level, *where)
            return remote(spot, spot, send.at[k], recv.at[k], axis, index)

        for peer in rep_peers:
            rep_copy(*peer).start()

    def adjoint(j):
        for k in range(cols - 1):
            grad_wait(j, k)
        secs[j] = dot(at[...], grads[j]).astype(BF16)
        for n, s in enumerate(OTHERS):
            @pl.when(inside(r + (s - HALF)))
            def _():
                sec_copy(j, n, s).start()

    def sec_copy(j, n, s):
        return remote(secs.at[j, sec(s), :], landed.at[j, n], ss.at[j, n], sr.at[j, n], "row", r + (s - HALF))

    def finish(j):
        total = secs[j, sec(HALF), :].astype(F32)
        for n, s in enumerate(OTHERS):
            @pl.when(inside(r - (s - HALF)))
            def _():
                sec_copy(j, n, s).wait_recv()
        for n in range(len(OTHERS)):
            total = total + landed[j, n].astype(F32)
        gfeat[0, :, j * wide : (j + 1) * wide] = total.astype(BF16)

    def rep_stage():
        for peer in rep_peers:
            rep_copy(*peer).wait_recv()
        total = mine[piece(rep_rows, p), :].astype(F32)
        for k in range(reps - 1):
            total = total + rep_in[k].astype(F32)
        row_out[...] = total.astype(BF16)
        for peer in row_peers:
            row_copy(*peer).start()

    def row_stage():
        for peer in row_peers:
            row_copy(*peer).wait_recv()
        total = row_out[piece(row_rows, r), :].astype(F32)
        for k in range(rows - 1):
            total = total + row_in[k].astype(F32)
        col_out[...] = total.astype(BF16)
        for peer in col_peers:
            col_copy(*peer).start()

    def col_stage():
        for peer in col_peers:
            col_copy(*peer).wait_recv()
        total = col_out[piece(col_rows, c), :].astype(F32)
        for k in range(cols - 1):
            total = total + col_in[k].astype(F32)
        place(0, p, r, c)[...] = total.astype(BF16)
        for peer in col_peers:
            back_copy(0, *peer).start()

    def back_stage(level, peers, then):
        for peer in peers:
            back_copy(level, *peer, arriving=True).wait_recv()
        for peer in then:
            back_copy(level + 1, *peer).start()

    if fused:
        rep_stage()
    for j in range(CHUNKS):
        adjoint(j)
        if fused and j == CHUNKS // 2:
            row_stage()
    if fused:
        col_stage()
    for j in range(CHUNKS):
        finish(j)
        if fused and j == CHUNKS // 2:
            back_stage(0, col_peers, row_peers)
    if fused:
        back_stage(1, row_peers, rep_peers)
        back_stage(2, rep_peers, [])
        gweight[...] = full[...].astype(F32)

    for j in range(CHUNKS):
        for n, s in enumerate(OTHERS):
            @pl.when(inside(r - (s - HALF)))
            def _():
                x_copy(j, n, s).wait_send()

            @pl.when(inside(r + (s - HALF)))
            def _():
                sec_copy(j, n, s).wait_send()
        for peer in col_peers:
            part_copy(j, *peer).wait_send()
            grad_copy(j, *peer).wait_send()
    if fused:
        for peer in rep_peers:
            rep_copy(*peer).wait_send()
            back_copy(2, *peer).wait_send()
        for peer in row_peers:
            row_copy(*peer).wait_send()
            back_copy(1, *peer).wait_send()
        for peer in col_peers:
            col_copy(*peer).wait_send()
            back_copy(0, *peer).wait_send()


def solution(mesh):
    rows, cols, reps = (mesh.shape[name] for name in ("row", "col", "rep"))

    def body(feat, cot, w, vals, touts, tins, tcount):
        span, width = feat.shape[1:]
        edge = vals.shape[-1]
        wide = width // CHUNKS
        fused = width % (16 * rows * cols * reps) == 0
        rep_rows = width // reps if fused else 16
        row_rows = rep_rows // rows if fused else 16
        col_rows = row_rows // cols if fused else 16
        few = lambda n: max(1, n - 1)
        vmem = pl.BlockSpec(memory_space=pltpu.VMEM)
        smem = pl.BlockSpec(memory_space=pltpu.SMEM)
        sems = lambda *shape: [pltpu.SemaphoreType.DMA(shape)] * 2
        result = pl.pallas_call(
            functools.partial(kernel, rows, cols, reps, fused),
            out_shape=(
                jax.ShapeDtypeStruct(feat.shape, BF16),
                jax.ShapeDtypeStruct(feat.shape, BF16),
                jax.ShapeDtypeStruct(w.shape, F32),
            ),
            in_specs=[vmem] * 4 + [smem] * 3,
            out_specs=(vmem,) * 3,
            scratch_shapes=[
                pltpu.VMEM((cols * edge, SECTIONS * edge), BF16),
                pltpu.VMEM((SECTIONS * edge, cols * edge), BF16),
                pltpu.VMEM((CHUNKS, SECTIONS * span, wide), BF16),
                pltpu.VMEM((CHUNKS, cols * span, wide), BF16),
                pltpu.VMEM((CHUNKS, few(cols), span, wide), BF16),
                pltpu.VMEM((span, width), BF16),
                pltpu.VMEM((CHUNKS, cols * span, wide), BF16),
                pltpu.VMEM((CHUNKS, SECTIONS * span, wide), BF16),
                pltpu.VMEM((CHUNKS, len(OTHERS), span, wide), BF16),
                pltpu.VMEM(w.shape if fused else (16, width), BF16),
                pltpu.VMEM((few(reps), rep_rows, width), BF16),
                pltpu.VMEM((rep_rows, width), BF16),
                pltpu.VMEM((few(rows) if fused else 1, row_rows, width), BF16),
                pltpu.VMEM((row_rows, width), BF16),
                pltpu.VMEM((few(cols), col_rows, width), BF16),
                pltpu.VMEM(w.shape if fused else (16, width), BF16),
                *sems(CHUNKS, len(OTHERS)),
                *sems(CHUNKS, few(cols)),
                *sems(CHUNKS, few(cols)),
                *sems(CHUNKS, len(OTHERS)),
                *(sems(few(reps)) + sems(few(rows) if fused else 1) + sems(few(cols))) * 2,
            ],
            compiler_params=pltpu.CompilerParams(
                collective_id=0, has_side_effects=True, vmem_limit_bytes=48 * 2**20
            ),
        )(feat, cot, w, vals, touts, tins, tcount)
        if fused:
            return result
        return (*result[:2], lax.psum(result[2], ("row", "col", "rep")))

    spread = ("row", "col")
    return jax.shard_map(
        body,
        mesh=mesh,
        in_specs=(
            P("rep", spread, None), P("rep", spread, None), P(), P("rep", spread, None, None),
            P("rep", spread), P("rep", spread), P("rep", spread),
        ),
        out_specs=(P("rep", spread, None), P("rep", spread, None), P()),
        check_vma=False,
    )
```

```python
import functools

import jax
import jax.numpy as jnp
from jax import lax
from jax.experimental import pallas as pl
from jax.experimental.pallas import tpu as pltpu
from jax.sharding import PartitionSpec as P

SECTIONS = 4
HALF = SECTIONS // 2
OTHERS = tuple(s for s in range(SECTIONS) if s != HALF)
CHUNKS = 4
AFTER = (
    "rep",
    "spread 1",
    "adjoint 0",
    "row",
    "spread 2",
    "adjoint 1",
    "col",
    "spread 3",
    "adjoint 2",
    "back0",
    "adjoint 3",
    "back1",
    "finish 0",
    "finish 1",
    "finish 2",
    "finish 3",
)
MESH = pl.DeviceIdType.MESH
F32, BF16 = jnp.float32, jnp.bfloat16


def remote(src, dst, send, recv, axis, index):
    return pltpu.make_async_remote_copy(
        src_ref=src, dst_ref=dst, send_sem=send, recv_sem=recv, device_id={axis: index}, device_id_type=MESH
    )


def dot(a, b, dims=((1,), (0,))):
    return lax.dot_general(a, b, (dims, ((), ())), preferred_element_type=F32)


def kernel(
    rows, cols, reps, fused,
    feat, cot_hbm, w_hbm, vals_hbm, touts, tins, tcount,
    out_hbm, gfeat_hbm, gweight_hbm,
    out, gfeat, out_sem, gfeat_sem, gweight_sem,
    cot, w, vals, feat_sem, cot_sem, w_sem, vals_sem,
    a, at, x, part, arrived, hid, grads, secs, landed,
    mine, rep_in, row_out, row_in, col_out, col_in, full,
    xs, xr, ps, pr, gs, gr, ss, sr, rs, rr, ws, wr, cs, cr, rs2, rr2, ws2, wr2, cs2, cr2,
):
    r, c, p = lax.axis_index("row"), lax.axis_index("col"), lax.axis_index("rep")
    span, width = feat.shape[1:]
    wide = width // CHUNKS
    edge = vals.shape[-1]
    slots = vals.shape[1]
    own = pl.ds(pl.multiple_of(c * span, span), span)

    def sec(s):
        return pl.ds(s * span, span)

    def cut(j):
        return pl.ds(j * wide, wide)

    def inside(index):
        return jnp.logical_and(index >= 0, index < rows)

    def ring(axis, me, count):
        return [(k - 1, axis, lax.rem(me + k, count)) for k in range(1, count)]

    col_peers = ring("col", c, cols)
    row_peers = ring("row", r, rows) if fused else []
    rep_peers = ring("rep", p, reps) if fused else []

    loads = [pltpu.make_async_copy(feat.at[0, :, cut(j)], x.at[j, sec(HALF), :], feat_sem.at[j]) for j in range(CHUNKS)]
    vals_load = pltpu.make_async_copy(vals_hbm, vals, vals_sem.at[0])
    w_load = pltpu.make_async_copy(w_hbm, w, w_sem.at[0])
    cot_load = pltpu.make_async_copy(cot_hbm, cot, cot_sem.at[0])
    for load in [vals_load, *loads, w_load, cot_load]:
        load.start()

    barrier = pltpu.get_barrier_semaphore()
    for _, axis, index in col_peers + row_peers + rep_peers:
        pl.semaphore_signal(barrier, inc=1, device_id={axis: index}, device_id_type=MESH)
    if not fused:
        for d in (-2, -1, 1, 2):
            @pl.when(inside(r + d))
            def _():
                pl.semaphore_signal(barrier, inc=1, device_id={"row": r + d}, device_id_type=MESH)
        for d in (-2, -1, 1, 2):
            @pl.when(inside(r + d))
            def _():
                pl.semaphore_wait(barrier, 1)
    pl.semaphore_wait(barrier, len(col_peers + row_peers + rep_peers))

    def x_copy(j, n, s):
        return remote(feat.at[0, :, cut(j)], x.at[j, sec(s), :], xs.at[j, n], xr.at[j, n], "row", r - (s - HALF))

    for j in range(CHUNKS):
        for n, s in enumerate(OTHERS):
            @pl.when(inside(r - (s - HALF)))
            def _():
                x_copy(j, n, s).start()

    for j in range(CHUNKS):
        for n, s in enumerate(OTHERS):
            @pl.when(jnp.logical_not(inside(r + (s - HALF))))
            def _():
                x[j, sec(s), :] = jnp.zeros((span, wide), BF16)

            @pl.when(jnp.logical_not(inside(r - (s - HALF))))
            def _():
                landed[j, n] = jnp.zeros((span, wide), BF16)

    count = tcount[0, 0]
    one, zero = jnp.float32(1), jnp.float32(0)
    hot_out = [[jnp.where(touts[0, t] == o, one, zero) for o in range(cols)] for t in range(slots)]
    hot_in = [
        [jnp.where(jnp.logical_and(tins[0, t] == i, t < count), one, zero) for i in range(SECTIONS)]
        for t in range(slots)
    ]
    strip = 16
    vals_load.wait()

    @pl.loop(0, edge // strip)
    def _(step):
        at_row = pl.multiple_of(step * strip, strip)
        total = [[jnp.zeros((strip, edge), F32) for _ in range(SECTIONS)] for _ in range(cols)]
        for t in range(slots):
            v = vals[0, t, pl.ds(at_row, strip), :].astype(F32)
            for i in range(SECTIONS):
                picked = v * hot_in[t][i]
                for o in range(cols):
                    total[o][i] = total[o][i] + picked * hot_out[t][o]
        for o in range(cols):
            for i in range(SECTIONS):
                a[pl.ds(o * edge + at_row, strip), i * edge : (i + 1) * edge] = total[o][i].astype(BF16)

    def part_copy(j, k, axis, index):
        rows_of = pl.ds(pl.multiple_of(index * span, span), span)
        return remote(part.at[j, rows_of, :], arrived.at[j, k], ps.at[j, k], pr.at[j, k], axis, index)

    for j in range(CHUNKS):
        for n, s in enumerate(OTHERS):
            @pl.when(inside(r + (s - HALF)))
            def _():
                x_copy(j, n, s).wait_recv()
        loads[j].wait()
        part[j] = dot(a[...], x[j]).astype(BF16)
        for peer in col_peers:
            part_copy(j, *peer).start()

    at[...] = a[...].astype(F32).T.astype(BF16)

    w_load.wait()
    cot_load.wait()
    pre = jnp.zeros((span, width), F32)
    for j in range(CHUNKS):
        for peer in col_peers:
            part_copy(j, *peer).wait_recv()
        summed = part[j, own, :].astype(F32)
        for k in range(cols - 1):
            summed = summed + arrived[j, k].astype(F32)
        summed = summed.astype(BF16)
        hid[:, j * wide : (j + 1) * wide] = summed
        pre = pre + dot(summed, w[j * wide : (j + 1) * wide, :])

    sigma = jax.nn.sigmoid(pre)
    dpre = (cot[0].astype(F32) * sigma * (1.0 + pre * (1.0 - sigma))).astype(BF16)

    def grad_copy(j, k, axis, index):
        return remote(grads.at[j, own, :], grads.at[j, own, :], gs.at[j, k], gr.at[j, k], axis, index)

    def grad_wait(j, k):
        source = pl.ds(pl.multiple_of(lax.rem(c + cols - 1 - k, cols) * span, span), span)
        remote(grads.at[j, source, :], grads.at[j, source, :], gs.at[j, k], gr.at[j, k], "col", col_peers[k][2]).wait_recv()

    def spread(j):
        grads[j, own, :] = dot(dpre, w[j * wide : (j + 1) * wide, :], ((1,), (1,))).astype(BF16)
        for peer in col_peers:
            grad_copy(j, *peer).start()
    spread(0)
    scale = float(span * rows * cols * reps) ** -0.5
    term = dot(hid[...].astype(F32).T.astype(BF16), dpre) * scale
    if not fused:
        full[...] = term
        whole_store = pltpu.make_async_copy(full, gweight_hbm, gweight_sem.at[0])
        whole_store.start()
    else:
        mine[...] = term.astype(BF16)
        rep_rows = width // reps
        row_rows = rep_rows // rows
        col_rows = row_rows // cols

        def piece(size, index):
            return pl.ds(pl.multiple_of(index * size, size), size)

        def rep_copy(k, axis, index):
            return remote(mine.at[piece(rep_rows, index), :], rep_in.at[k], rs.at[k], rr.at[k], axis, index)

        def row_copy(k, axis, index):
            return remote(row_out.at[piece(row_rows, index), :], row_in.at[k], ws.at[k], wr.at[k], axis, index)

        def col_copy(k, axis, index):
            return remote(col_out.at[piece(col_rows, index), :], col_in.at[k], cs.at[k], cr.at[k], axis, index)

        def place(level, p, r, c):
            start = p * rep_rows
            if level < 2:
                start = start + r * row_rows
            if level < 1:
                start = start + c * col_rows
            size = (col_rows, row_rows, rep_rows)[level]
            return full.at[pl.ds(pl.multiple_of(start, size), size), :]

        def back_copy(level, k, axis, index, arriving=False):
            send, recv = ((cs2, cr2), (ws2, wr2), (rs2, rr2))[level]
            where = [p, r, c]
            if arriving:
                which = ("rep", "row", "col").index(axis)
                total = (reps, rows, cols)[which]
                where[which] = lax.rem(where[which] + total - 1 - k, total)
            spot = place(level, *where)
            return remote(spot, spot, send.at[k], recv.at[k], axis, index)

        for peer in rep_peers:
            rep_copy(*peer).start()

    def adjoint(j):
        for k in range(cols - 1):
            grad_wait(j, k)
        secs[j] = dot(at[...], grads[j]).astype(BF16)
        for n, s in enumerate(OTHERS):
            @pl.when(inside(r + (s - HALF)))
            def _():
                sec_copy(j, n, s).start()

    def sec_copy(j, n, s):
        return remote(secs.at[j, sec(s), :], landed.at[j, n], ss.at[j, n], sr.at[j, n], "row", r + (s - HALF))

    def finish(j):
        total = secs[j, sec(HALF), :].astype(F32)
        for n, s in enumerate(OTHERS):
            @pl.when(inside(r - (s - HALF)))
            def _():
                sec_copy(j, n, s).wait_recv()
        for n in range(len(OTHERS)):
            total = total + landed[j, n].astype(F32)
        gfeat[j] = total.astype(BF16)
        gfeat_store(j).start()

    def gfeat_store(j):
        return pltpu.make_async_copy(gfeat.at[j], gfeat_hbm.at[0, :, cut(j)], gfeat_sem.at[j])

    def rep_stage():
        for peer in rep_peers:
            rep_copy(*peer).wait_recv()
        total = mine[piece(rep_rows, p), :].astype(F32)
        for k in range(reps - 1):
            total = total + rep_in[k].astype(F32)
        row_out[...] = total.astype(BF16)
        for peer in row_peers:
            row_copy(*peer).start()

    def row_stage():
        for peer in row_peers:
            row_copy(*peer).wait_recv()
        total = row_out[piece(row_rows, r), :].astype(F32)
        for k in range(rows - 1):
            total = total + row_in[k].astype(F32)
        col_out[...] = total.astype(BF16)
        for peer in col_peers:
            col_copy(*peer).start()

    def col_stage():
        for peer in col_peers:
            col_copy(*peer).wait_recv()
        total = col_out[piece(col_rows, c), :].astype(F32)
        for k in range(cols - 1):
            total = total + col_in[k].astype(F32)
        place(0, p, r, c)[...] = total.astype(BF16)
        for peer in col_peers:
            back_copy(0, *peer).start()

    def back_stage(level, peers, then):
        for peer in peers:
            back_copy(level, *peer, arriving=True).wait_recv()
        for peer in then:
            back_copy(level + 1, *peer).start()

    def half_store(n, half):
        return pltpu.make_async_copy(
            full.at[piece(rep_rows, half), :], gweight_hbm.at[piece(rep_rows, half), :], gweight_sem.at[n]
        )

    out[0] = (pre * sigma).astype(BF16)
    out_store = pltpu.make_async_copy(out, out_hbm, out_sem.at[0])
    out_store.start()

    stages = {
        "spread": spread,
        "adjoint": adjoint,
        "finish": finish,
        "rep": rep_stage,
        "row": row_stage,
        "col": col_stage,
        "back0": lambda: back_stage(0, col_peers, row_peers),
        "back1": lambda: back_stage(1, row_peers, rep_peers),
    }
    for name in AFTER:
        stage, _, index = name.partition(" ")
        if index:
            stages[stage](int(index))
        elif fused:
            stages[stage]()
    if fused:
        half_store(0, p).start()
    if fused:
        back_stage(2, rep_peers, [])
        for k in range(reps - 1):
            half_store(k + 1, lax.rem(p + k + 1, reps)).start()
        for k in range(reps):
            half_store(k, lax.rem(p + k, reps)).wait()
    else:
        whole_store.wait()
    out_store.wait()
    for j in range(CHUNKS):
        gfeat_store(j).wait()

    for j in range(CHUNKS):
        for n, s in enumerate(OTHERS):
            @pl.when(inside(r - (s - HALF)))
            def _():
                x_copy(j, n, s).wait_send()

            @pl.when(inside(r + (s - HALF)))
            def _():
                sec_copy(j, n, s).wait_send()
        for peer in col_peers:
            part_copy(j, *peer).wait_send()
            grad_copy(j, *peer).wait_send()
    if fused:
        for peer in rep_peers:
            rep_copy(*peer).wait_send()
            back_copy(2, *peer).wait_send()
        for peer in row_peers:
            row_copy(*peer).wait_send()
            back_copy(1, *peer).wait_send()
        for peer in col_peers:
            col_copy(*peer).wait_send()
            back_copy(0, *peer).wait_send()


def solution(mesh):
    rows, cols, reps = (mesh.shape[name] for name in ("row", "col", "rep"))

    def body(feat, cot, w, vals, touts, tins, tcount):
        span, width = feat.shape[1:]
        edge = vals.shape[-1]
        wide = width // CHUNKS
        fused = width % (16 * rows * cols * reps) == 0
        rep_rows = width // reps if fused else 16
        row_rows = rep_rows // rows if fused else 16
        col_rows = row_rows // cols if fused else 16
        few = lambda n: max(1, n - 1)
        hbm = pl.BlockSpec(memory_space=pltpu.HBM)
        smem = pl.BlockSpec(memory_space=pltpu.SMEM)
        sems = lambda *shape: [pltpu.SemaphoreType.DMA(shape)] * 2
        result = pl.pallas_call(
            functools.partial(kernel, rows, cols, reps, fused),
            out_shape=(
                jax.ShapeDtypeStruct(feat.shape, BF16),
                jax.ShapeDtypeStruct(feat.shape, BF16),
                jax.ShapeDtypeStruct(w.shape, BF16 if fused else F32),
            ),
            in_specs=[hbm] * 4 + [smem] * 3,
            out_specs=(hbm,) * 3,
            scratch_shapes=[
                pltpu.VMEM(feat.shape, BF16),
                pltpu.VMEM((CHUNKS, span, wide), BF16),
                pltpu.SemaphoreType.DMA((1,)),
                pltpu.SemaphoreType.DMA((CHUNKS,)),
                pltpu.SemaphoreType.DMA((reps,)),
                pltpu.VMEM(cot.shape, BF16),
                pltpu.VMEM(w.shape, BF16),
                pltpu.VMEM(vals.shape, BF16),
                pltpu.SemaphoreType.DMA((CHUNKS,)),
                pltpu.SemaphoreType.DMA((1,)),
                pltpu.SemaphoreType.DMA((1,)),
                pltpu.SemaphoreType.DMA((1,)),
                pltpu.VMEM((cols * edge, SECTIONS * edge), BF16),
                pltpu.VMEM((SECTIONS * edge, cols * edge), BF16),
                pltpu.VMEM((CHUNKS, SECTIONS * span, wide), BF16),
                pltpu.VMEM((CHUNKS, cols * span, wide), BF16),
                pltpu.VMEM((CHUNKS, few(cols), span, wide), BF16),
                pltpu.VMEM((span, width), BF16),
                pltpu.VMEM((CHUNKS, cols * span, wide), BF16),
                pltpu.VMEM((CHUNKS, SECTIONS * span, wide), BF16),
                pltpu.VMEM((CHUNKS, len(OTHERS), span, wide), BF16),
                pltpu.VMEM(w.shape if fused else (16, width), BF16),
                pltpu.VMEM((few(reps), rep_rows, width), BF16),
                pltpu.VMEM((rep_rows, width), BF16),
                pltpu.VMEM((few(rows) if fused else 1, row_rows, width), BF16),
                pltpu.VMEM((row_rows, width), BF16),
                pltpu.VMEM((few(cols), col_rows, width), BF16),
                pltpu.VMEM(w.shape, BF16 if fused else F32),
                *sems(CHUNKS, len(OTHERS)),
                *sems(CHUNKS, few(cols)),
                *sems(CHUNKS, few(cols)),
                *sems(CHUNKS, len(OTHERS)),
                *(sems(few(reps)) + sems(few(rows) if fused else 1) + sems(few(cols))) * 2,
            ],
            compiler_params=pltpu.CompilerParams(
                collective_id=0, has_side_effects=True, vmem_limit_bytes=58 * 2**20
            ),
        )(feat, cot, w, vals, touts, tins, tcount)
        if fused:
            return (*result[:2], result[2].astype(F32))
        return (*result[:2], lax.psum(result[2], ("row", "col", "rep")))

    spread = ("row", "col")
    return jax.shard_map(
        body,
        mesh=mesh,
        in_specs=(
            P("rep", spread, None), P("rep", spread, None), P(), P("rep", spread, None, None),
            P("rep", spread), P("rep", spread), P("rep", spread),
        ),
        out_specs=(P("rep", spread, None), P("rep", spread, None), P()),
        check_vma=False,
    )
```
